128 devices in a mesh: row: 8 (over y, x_hi), col: 16 (over x_lo, z, core).
Axes of the slice: x: 4 (x_hi: 2, x_lo: 2; x = x_hi * 2 + x_lo), y: 4, z: 4, core: 2. Of those that a mesh axis runs over, the one named last changes fastest.
Arguments:
- amplitudes: float32 [64, 131072], P(None, ('row', 'col')), may hold values from -6 to 6
- ladder_ints: float32 [131072, 4096], P('row', 'col'), may hold values from -0.046875 to 0.046875
- tile_mask: int32 [2048, 64], replicated, may hold values from 0 to 1, as said below
Outputs:
- ladder: float32 [64, 4096], P(None, 'col')
The draws below stay inside these ranges and needn't reach their ends.
Inputs may be any that keep to these rules, and one draw needn't show every extreme that they name: `tile_mask`: among each aligned run of 16 cd tile rows (one device's amplitude tiles), at most 8 rows hold a nonzero tile.
All inputs are finite; a program needn't handle non-finite values.
Results may differ from the reference program's by a relative error of at most 0.0001.
Values sent between devices are 32-bit elements; how exact they have to be, the bound alone decides.
A program may use at most 192 MiB of HBM per device.

```python
import jax
import jax.numpy as jnp
from jax import lax

PAIRS = 64
TILE = 64
GROUP = 16
LIVE = 8
CDT_DEV = 256
CDT = 2048
CD = 131072
ABT = 64
AB = 4096
N_ROW = 8


def draw_tile_mask(key, part):
    key = jax.random.fold_in(key, 11)
    key_rank, key_level, key_bits, key_force = jax.random.split(key, 4)
    groups = CDT // GROUP
    scores = jax.random.randint(key_rank, (groups, GROUP), 0, 1 << 20) * GROUP + jnp.arange(GROUP, dtype=jnp.int32)[None, :]
    ranks = jnp.argsort(jnp.argsort(scores, axis=1, stable=True), axis=1, stable=True)
    is_live = ranks < LIVE
    levels = jax.random.randint(key_level, (groups, 1, 1), 0, 4)
    coin = jax.random.randint(key_bits, (groups, GROUP, ABT), 0, 8)
    switched = coin < levels + 2
    forced = jax.random.randint(key_force, (groups, GROUP), 0, ABT)
    onehot = jnp.arange(ABT, dtype=jnp.int32)[None, None, :] == forced[:, :, None]
    result = is_live[:, :, None] & (switched | onehot)
    return result.reshape(CDT, ABT).astype(jnp.int32)


def strengthened(entries, key, source, target, shards_of, factor):
    owner, partner = [(jnp.arange(entries.shape[axis_at]) // (entries.shape[axis_at] // shards_of)).reshape([-1 if axis == axis_at else 1 for axis in range(entries.ndim)]) for axis_at in (source, target)]
    chosen = jax.random.permutation(key, shards_of)[partner]
    strong = (owner == chosen) | (owner == (partner + shards_of // 2) % shards_of)
    return jnp.where(strong, factor * entries, entries)


def block_levels(rng, dims, pieces, smallest, high):
    factor_of = 1.0
    for axis_at, parts in pieces:
        draws = jax.random.uniform(jax.random.fold_in(jax.random.fold_in(rng, 6), axis_at), (parts,), jnp.float32, smallest / len(pieces), high / len(pieces))
        factor_of = factor_of * jnp.repeat(jnp.exp(draws), dims[axis_at] // parts).reshape((-1,) + (1,) * (len(dims) - 1 - axis_at))
    return factor_of


def centred(rng, dims, scale, bound, pieces=(), kind=jnp.bfloat16):
    level = block_levels(rng, dims, pieces, -0.22, 0.18) if pieces else 1.0
    drawn = jax.random.normal(rng, dims, jnp.float32) * scale * level
    return jnp.minimum(jnp.maximum(drawn, -bound), bound).astype(kind)


def heavy_noise(stream_key, shape, width, bound, shards, heavy, kind=jnp.bfloat16):
    values = width * jax.random.normal(stream_key, shape, jnp.float32)
    if shards:
        values = values * block_levels(stream_key, shape, shards, -0.22, 0.18)
    return jnp.clip(strengthened(values, jax.random.fold_in(stream_key, 3), *heavy), -bound, bound).astype(kind)


def setup_inputs(seed: int = 0) -> dict:
    keys = jax.random.split(jax.random.key(seed), 4)
    amplitudes = centred(keys[0], (PAIRS, CD), 1.0, 6.0, ((1, 128),), jnp.float32)
    ladder_ints = heavy_noise(keys[1], (CD, AB), (CD // 4) ** -0.5, 0.046875, ((0, 8), (1, 16)), (0, 1, 16, 2.0), jnp.float32)
    tile_mask = draw_tile_mask(jax.random.fold_in(keys[3], 71), 0)
    return {"amplitudes": amplitudes, "ladder_ints": ladder_ints, "tile_mask": tile_mask}


def reference(amplitudes, ladder_ints, tile_mask):
    block_rows = CDT_DEV * TILE
    slabs = ladder_ints.reshape(N_ROW, block_rows, AB)
    masks = tile_mask.reshape(N_ROW, CDT_DEV, ABT)
    panels = amplitudes.reshape(PAIRS, N_ROW, block_rows).transpose(1, 0, 2)

    def step(running, blocks):
        panel, slab, mask_part = blocks
        masked = (slab.reshape(CDT_DEV, TILE, ABT, TILE) * mask_part[:, None, :, None].astype(slab.dtype)).reshape(block_rows, AB)
        return running + jnp.dot(panel, masked, precision=lax.Precision.HIGHEST, preferred_element_type=jnp.float32), None

    start_sum = jnp.zeros((PAIRS, AB), jnp.float32)
    ladder, unused = lax.scan(step, start_sum, (panels, slabs, masks))
    return ladder
```

```python
import functools

import jax
import jax.numpy as jnp
from jax import lax
from jax.experimental import pallas as pl
from jax.experimental.pallas import tpu as pltpu
from jax.sharding import PartitionSpec as P

TILE = 64
GROUP = 16
LIVE = 8
PIECES = 4
LANES = 128
MESH = pl.DeviceIdType.MESH

TREE_A = {(0, 0): "udx", (0, 1): "ux", (1, 0): "d", (1, 1): "u"}
TREE_M = {(0, 0): "udx", (0, 3): "dx", (1, 0): "u", (1, 3): "d"}
TREES = (TREE_A, TREE_M, TREE_A, TREE_M)

ROUNDS = (((0, 1), (0, 3), (1, 0)), ((0, 2), (1, 1), (1, 3)), ((1, 2),))


def kernel(rows, t_hbm, v_hbm, m_hbm, o_ref, t_in, m_in, list_v, list_s, v_hi, v_lo, t_all, acc, red, fin,
           in_sem, v_sem, out_sem, got_sem, red_out, red_got, fin_out, fin_got, *v_in):
    row = lax.axis_index("row")
    col = lax.axis_index("col")
    core = lax.rem(col, 2)
    z = lax.rem(lax.div(col, 2), 4)
    x_lo = lax.div(col, 8)

    def col_of(dx, dz, dc):
        return lax.rem(x_lo + dx, 2) * 8 + lax.rem(z + dz, 4) * 2 + lax.rem(core + dc, 2)

    link = {"u": col_of(0, 1, 0), "d": col_of(0, 3, 0), "x": col_of(1, 0, 0), "s": col_of(0, 0, 1)}

    mask_copy = pltpu.make_async_copy(
        m_hbm.at[:, pl.ds(pl.multiple_of(row * 256, 256), 256)], m_in, in_sem.at[0])
    mask_copy.start()
    t_copy = pltpu.make_async_copy(t_hbm, t_in, in_sem.at[1])
    t_copy.start()

    order = [(0, 0)] + [e for rnd in ROUNDS for e in rnd]
    owner = {(e, dc): col_of(e[0], (4 - e[1]) % 4, dc) for e in order for dc in (0, 1)}
    v_of = dict(zip(owner, v_in))
    v_copies = {}
    for n, at in enumerate(owner):
        v_copies[at] = pltpu.make_async_copy(
            v_hbm.at[pl.ds(pl.multiple_of(owner[at] * 1024, 1024), 1024), :], v_of[at], v_sem.at[n])
        v_copies[at].start()

    barrier = pltpu.get_barrier_semaphore()
    for to in link.values():
        pl.semaphore_signal(barrier, inc=1, device_id={"col": to}, device_id_type=MESH)
    for k in range(1, rows):
        pl.semaphore_signal(barrier, inc=1, device_id={"row": lax.rem(row + k, rows)}, device_id_type=MESH)

    mask_copy.wait()
    live = jnp.broadcast_to(jnp.max(m_in[...], axis=0, keepdims=True), (8, 256))
    lane = lax.broadcasted_iota(jnp.int32, (8, 256), 1)
    slot = lax.broadcasted_iota(jnp.int32, (8, 256), 0)
    tile = lane & 15
    count = live
    for s in (1, 2, 4, 8):
        count = count + jnp.where(tile >= s, pltpu.roll(count, s, 1), 0)
    place = jnp.where(live > 0, count - 1, 15 - tile + count)
    mine = m_in[pl.ds(pl.multiple_of(lax.div(col, 2) * 8, 8), 8), :]
    bit = slot - lax.rem(col, 2) * 4
    weight = jnp.where(bit == 0, 16, jnp.where(bit == 1, 32, jnp.where(bit == 2, 64, jnp.where(bit == 3, 128, 0))))
    code = jnp.sum(mine * weight, axis=0, keepdims=True)
    entry = jnp.where(place == slot, tile + code, 0)
    for s in (1, 2, 4, 8):
        entry = entry + pltpu.roll(entry, 256 - s, 1)
    list_v[...] = entry
    list_copy = pltpu.make_async_copy(list_v, list_s, in_sem.at[2])
    list_copy.start()
    list_copy.wait()
    t_copy.wait()

    left = lax.broadcasted_iota(jnp.int32, (TILE, LANES), 1) < TILE
    for p in range(PIECES):
        halves = []
        for h in (0, 1):
            at = list_s[2 * p + h, col * GROUP] & 15
            block = t_in[:, pl.ds((at >> 1) * LANES, LANES)]
            odd = jnp.full((TILE, LANES), at, jnp.int32) & 1
            halves.append(jnp.where(odd != h, pltpu.roll(block, TILE, 1), block))
        t_all[col, p] = jnp.where(left, halves[0], halves[1])

    pl.semaphore_wait(barrier, len(link) + rows - 1)

    sent = []

    def piece(s, p, to, n):
        return pltpu.make_async_remote_copy(
            src_ref=t_all.at[s, p], dst_ref=t_all.at[s, p], send_sem=out_sem.at[n],
            recv_sem=got_sem.at[s * PIECES + p], device_id={"col": to}, device_id_type=MESH)

    def send(s, p, to):
        copy = piece(s, p, to, len(sent))
        copy.start()
        sent.append(copy)

    def arrive(s, p):
        piece(s, p, link["s"], 0).wait_recv()

    for p in range(PIECES):
        for way in TREES[p][0, 0]:
            send(col, p, link[way])
    for p in range(PIECES):
        send(col, p, link["s"])

    bits = 16 << lax.div(lax.broadcasted_iota(jnp.int32, (1, 256), 1), TILE)

    def prepare(e, dc):
        s = owner[e, dc]
        v_copies[e, dc].wait()

        def one(k, carry):
            at = list_s[k, s * GROUP]
            tile_rows = v_of[e, dc][pl.ds((at & 15) * TILE, TILE), :]
            tile_rows = jnp.where((jnp.full((1, 256), at, jnp.int32) & bits) != 0, tile_rows, 0.0)
            high = tile_rows.astype(jnp.bfloat16)
            low = (tile_rows - high.astype(jnp.float32)).astype(jnp.bfloat16)
            to = pl.ds(pl.multiple_of(k * TILE, TILE), TILE)
            v_hi[s, to, :] = high
            v_lo[s, to, :] = low
            return carry

        lax.fori_loop(0, LIVE, one, 0)

    def multiply(e, dc):
        s = owner[e, dc]
        t = jnp.concatenate([t_all[s, p] for p in range(PIECES)], axis=1)
        high = t.astype(jnp.bfloat16)
        low = (t - high.astype(jnp.float32)).astype(jnp.bfloat16)
        both = jnp.dot(jnp.concatenate([high, low], axis=0), v_hi[s], preferred_element_type=jnp.float32)
        more = jnp.dot(high, v_lo[s], preferred_element_type=jnp.float32)
        acc[...] += both[:64] + (both[64:] + more)

    acc[...] = jnp.zeros_like(acc)
    prepare((0, 0), 0)
    prepare((0, 0), 1)
    multiply((0, 0), 0)

    last = ((0, 0),)
    for rnd in ROUNDS:
        for p in range(PIECES):
            for e in rnd:
                s = owner[e, 0]
                arrive(s, p)
                for way in TREES[p].get(e, ""):
                    send(s, p, link[way])
                send(s, p, link["s"])
            if p < len(rnd):
                prepare(rnd[p], 0)
                prepare(rnd[p], 1)
        for e in last:
            for p in range(PIECES):
                arrive(owner[e, 1], p)
            multiply(e, 1)
        for e in rnd:
            multiply(e, 0)
        last = rnd
    for e in last:
        for p in range(PIECES):
            arrive(owner[e, 1], p)
        multiply(e, 1)

    def part(q):
        return pl.ds(pl.multiple_of(q * 8, 8), 8)

    red_copies, fin_copies = [], []
    for k in range(1, rows):
        to = lax.rem(row + k, rows)
        copy = pltpu.make_async_remote_copy(
            src_ref=acc.at[part(to)], dst_ref=red.at[k], send_sem=red_out.at[k], recv_sem=red_got.at[k],
            device_id={"row": to}, device_id_type=MESH)
        copy.start()
        red_copies.append(copy)
    total = acc[part(row), :]
    for copy in red_copies:
        copy.wait_recv()
    for k in range(1, rows):
        total = total + red[k]
    fin[row] = total
    for k in range(1, rows):
        to = lax.rem(row + k, rows)
        copy = pltpu.make_async_remote_copy(
            src_ref=fin.at[row], dst_ref=fin.at[row], send_sem=fin_out.at[k], recv_sem=fin_got.at[row],
            device_id={"row": to}, device_id_type=MESH)
        copy.start()
        fin_copies.append(copy)
    o_ref[part(row), :] = total
    for k in range(1, rows):
        q = lax.rem(row + k, rows)
        pltpu.make_async_remote_copy(
            src_ref=fin.at[q], dst_ref=fin.at[q], send_sem=fin_out.at[k], recv_sem=fin_got.at[q],
            device_id={"row": q}, device_id_type=MESH).wait_recv()
        o_ref[part(q), :] = fin[q]

    for copy in sent + red_copies + fin_copies:
        copy.wait_send()


def per_device(rows, amplitudes, ladder_ints, tile_mask):
    n_sent = sum(len(ways) for tree in TREES for ways in tree.values()) + 8 * PIECES
    return pl.pallas_call(
        functools.partial(kernel, rows),
        out_shape=jax.ShapeDtypeStruct((64, 256), jnp.float32),
        in_specs=[pl.BlockSpec(memory_space=pl.ANY)] * 3,
        out_specs=pl.BlockSpec(memory_space=pltpu.VMEM),
        scratch_shapes=[
            pltpu.VMEM((64, 1024), jnp.float32),
            pltpu.VMEM((64, 256), jnp.int32),
            pltpu.VMEM((8, 256), jnp.int32),
            pltpu.SMEM((8, 256), jnp.int32),
            pltpu.VMEM((16, LIVE * TILE, 256), jnp.bfloat16),
            pltpu.VMEM((16, LIVE * TILE, 256), jnp.bfloat16),
            pltpu.VMEM((16, PIECES, 64, LANES), jnp.float32),
            pltpu.VMEM((64, 256), jnp.float32),
            pltpu.VMEM((rows, 8, 256), jnp.float32),
            pltpu.VMEM((rows, 8, 256), jnp.float32),
            pltpu.SemaphoreType.DMA((3,)),
            pltpu.SemaphoreType.DMA((16,)),
            pltpu.SemaphoreType.DMA((n_sent,)),
            pltpu.SemaphoreType.DMA((16 * PIECES,)),
            pltpu.SemaphoreType.DMA((rows,)),
            pltpu.SemaphoreType.DMA((rows,)),
            pltpu.SemaphoreType.DMA((rows,)),
            pltpu.SemaphoreType.DMA((rows,)),
        ] + [pltpu.VMEM((1024, 256), jnp.float32)] * 16,
        compiler_params=pltpu.CompilerParams(
            collective_id=0, has_side_effects=True, vmem_limit_bytes=60 * 1024 * 1024),
    )(amplitudes, ladder_ints, tile_mask.T)


def solution(mesh):
    in_specs = (P(None, ("row", "col")), P("row", "col"), P())
    out_specs = P(None, "col")
    return jax.shard_map(
        functools.partial(per_device, mesh.shape["row"]), mesh=mesh, in_specs=in_specs, out_specs=out_specs,
        check_vma=False)
```

```python
import functools

import jax
import jax.numpy as jnp
from jax import lax
from jax.experimental import pallas as pl
from jax.experimental.pallas import tpu as pltpu
from jax.sharding import PartitionSpec as P

TILE = 64
GROUP = 16
LIVE = 8
PIECES = 2
WIDTH = 256
MESH = pl.DeviceIdType.MESH

TREE = {(0, 1): "xs", (0, 3): "xs", (1, 0): "2s", (0, 2): "s", (1, 1): "s", (1, 3): "s", (1, 2): "s"}
FIRST = ((1, 0), (0, 1), (0, 3))
SECOND = ((1, 1), (1, 3), (1, 2))
ORDER = ((0, 0),) + FIRST + ((0, 2),) + SECOND
N_SENT = (4 + 1 + 3 + 7) * PIECES
ROUNDS = 3


def kernel(rows, t_hbm, v_hbm, m_hbm, o_ref, t_in, m_in, list_v, list_s, v_hi, v_lo, t_all, acc, red, fin,
           in_sem, v_sem, out_sem, got_sem, red_out, red_got, fin_out, fin_got, near_sem, *v_in):
    row = lax.axis_index("row")
    col = lax.axis_index("col")
    core = lax.rem(col, 2)
    z = lax.rem(lax.div(col, 2), 4)
    x_lo = lax.div(col, 8)
    y = lax.div(row, 2)
    x_hi = lax.rem(row, 2)

    def col_of(dx, dz, dc):
        return lax.rem(x_lo + dx, 2) * 8 + lax.rem(z + dz, 4) * 2 + lax.rem(core + dc, 2)

    def row_of(dy, dx):
        return lax.rem(y + dy, 4) * 2 + lax.rem(x_hi + dx, 2)

    link = {"u": col_of(0, 1, 0), "d": col_of(0, 3, 0), "2": col_of(0, 2, 0), "x": col_of(1, 0, 0),
            "s": col_of(0, 0, 1)}
    near = ({"row": row_of(1, 0)}, {"row": row_of(3, 0)}, {"col": link["x"]}, {"row": row_of(0, 1), "col": link["x"]})

    mask_copy = pltpu.make_async_copy(
        m_hbm.at[:, pl.ds(pl.multiple_of(row * 256, 256), 256)], m_in, in_sem.at[0])
    mask_copy.start()
    t_copy = pltpu.make_async_copy(t_hbm, t_in, in_sem.at[1])
    t_copy.start()

    barrier = pltpu.get_barrier_semaphore()
    for to in [{"col": link[way]} for way in "ud2s"] + list(near):
        pl.semaphore_signal(barrier, inc=1, device_id=to, device_id_type=MESH)

    owner = {(e, dc): col_of(e[0], (4 - e[1]) % 4, dc) for e in ORDER for dc in (0, 1)}
    v_of = dict(zip(owner, v_in))
    v_copies = {}
    for n, at in enumerate(owner):
        v_copies[at] = pltpu.make_async_copy(
            v_hbm.at[pl.ds(pl.multiple_of(owner[at] * 1024, 1024), 1024), :], v_of[at], v_sem.at[n])
        v_copies[at].start()

    mask_copy.wait()
    live = jnp.broadcast_to(jnp.max(m_in[...], axis=0, keepdims=True), (8, 256))
    lane = lax.broadcasted_iota(jnp.int32, (8, 256), 1)
    slot = lax.broadcasted_iota(jnp.int32, (8, 256), 0)
    tile = lane & 15
    count = live
    for s in (1, 2, 4, 8):
        count = count + jnp.where(tile >= s, pltpu.roll(count, s, 1), 0)
    place = jnp.where(live > 0, count - 1, 15 - tile + count)
    mine = m_in[pl.ds(pl.multiple_of(lax.div(col, 2) * 8, 8), 8), :]
    bit = slot - lax.rem(col, 2) * 4
    weight = jnp.where(bit == 0, 16, jnp.where(bit == 1, 32, jnp.where(bit == 2, 64, jnp.where(bit == 3, 128, 0))))
    code = jnp.sum(mine * weight, axis=0, keepdims=True)
    entry = jnp.where(place == slot, tile + code, 0)
    for s in (1, 2, 4, 8):
        entry = entry + pltpu.roll(entry, 256 - s, 1)
    list_v[...] = entry
    list_copy = pltpu.make_async_copy(list_v, list_s, in_sem.at[2])
    list_copy.start()
    list_copy.wait()
    t_copy.wait()

    left = lax.broadcasted_iota(jnp.int32, (64, 128), 1) < TILE
    for p in range(LIVE // 2):
        halves = []
        for h in (0, 1):
            at = list_s[2 * p + h, col * GROUP] & 15
            block = t_in[:, pl.ds((at >> 1) * 128, 128)]
            odd = jnp.full((64, 128), at, jnp.int32) & 1
            halves.append(jnp.where(odd != h, pltpu.roll(block, TILE, 1), block))
        t_all[col, p // 2, :, (p % 2) * 128:(p % 2) * 128 + 128] = jnp.where(left, halves[0], halves[1])

    pl.semaphore_wait(barrier, 8)

    sent = []

    def piece(s, p, to, n):
        return pltpu.make_async_remote_copy(
            src_ref=t_all.at[s, p], dst_ref=t_all.at[s, p], send_sem=out_sem.at[n],
            recv_sem=got_sem.at[s * PIECES + p], device_id={"col": to}, device_id_type=MESH)

    def send(s, p, ways):
        for way in ways:
            copy = piece(s, p, link[way], len(sent))
            copy.start()
            sent.append(copy)

    def arrive(e, dc, p):
        piece(owner[e, dc], p, link["s"], 0).wait_recv()

    for p in range(PIECES):
        send(col, p, "udx")
    for p in range(PIECES):
        send(col, p, "s2")

    def tell(n):
        for to in near:
            pl.semaphore_signal(near_sem.at[n], inc=1, device_id=to, device_id_type=MESH)

    def hear(n):
        pl.semaphore_wait(near_sem.at[n], len(near))

    tell(0)

    bits = 16 << lax.div(lax.broadcasted_iota(jnp.int32, (1, 256), 1), TILE)

    def prepare(e, dc):
        s = owner[e, dc]
        v_copies[e, dc].wait()

        def one(k, carry):
            at = list_s[k, s * GROUP]
            tile_rows = v_of[e, dc][pl.ds((at & 15) * TILE, TILE), :]
            tile_rows = jnp.where((jnp.full((1, 256), at, jnp.int32) & bits) != 0, tile_rows, 0.0)
            high = tile_rows.astype(jnp.bfloat16)
            low = (tile_rows - high.astype(jnp.float32)).astype(jnp.bfloat16)
            to = pl.ds(pl.multiple_of(k * TILE, TILE), TILE)
            v_hi[s, to, :] = high
            v_lo[s, to, :] = low
            return carry

        lax.fori_loop(0, LIVE, one, 0)

    def multiply(e, dc):
        s = owner[e, dc]
        t = jnp.concatenate([t_all[s, p] for p in range(PIECES)], axis=1)
        high = t.astype(jnp.bfloat16)
        low = (t - high.astype(jnp.float32)).astype(jnp.bfloat16)
        both = jnp.dot(jnp.concatenate([high, low], axis=0), v_hi[s], preferred_element_type=jnp.float32)
        more = jnp.dot(high, v_lo[s], preferred_element_type=jnp.float32)
        acc[...] += both[:64] + (both[64:] + more)

    def pass_on(e, p):
        arrive(e, 0, p)
        send(owner[e, 0], p, TREE[e])

    def sibling(e):
        for p in range(PIECES):
            arrive(e, 1, p)
        multiply(e, 1)

    acc[...] = jnp.zeros_like(acc)
    prepare((0, 0), 0)
    prepare((0, 0), 1)
    multiply((0, 0), 0)
    sibling((0, 0))
    for e in FIRST:
        prepare(e, 0)
        prepare(e, 1)
    hear(0)
    tell(1)
    for p in range(PIECES):
        for e in FIRST:
            pass_on(e, p)
    for e in ((0, 2),) + SECOND[:2]:
        prepare(e, 0)
        prepare(e, 1)
    for p in range(PIECES):
        pass_on((0, 2), p)
    hear(1)
    tell(2)
    for e in FIRST:
        multiply(e, 0)
    for e in SECOND[2:]:
        prepare(e, 0)
        prepare(e, 1)
    for e in FIRST:
        sibling(e)
    multiply((0, 2), 0)
    hear(2)
    for p in range(PIECES):
        for e in SECOND:
            pass_on(e, p)
    sibling((0, 2))
    for e in SECOND:
        multiply(e, 0)
    for e in SECOND:
        sibling(e)

    def part(q):
        return pl.ds(pl.multiple_of(q * 8, 8), 8)

    red_copies, fin_copies = [], []
    for k in range(1, rows):
        to = lax.rem(row + k, rows)
        copy = pltpu.make_async_remote_copy(
            src_ref=acc.at[part(to)], dst_ref=red.at[k], send_sem=red_out.at[k], recv_sem=red_got.at[k],
            device_id={"row": to}, device_id_type=MESH)
        copy.start()
        red_copies.append(copy)
    total = acc[part(row), :]
    for copy in red_copies:
        copy.wait_recv()
    for k in range(1, rows):
        total = total + red[k]
    fin[row] = total
    for k in range(1, rows):
        to = lax.rem(row + k, rows)
        copy = pltpu.make_async_remote_copy(
            src_ref=fin.at[row], dst_ref=fin.at[row], send_sem=fin_out.at[k], recv_sem=fin_got.at[row],
            device_id={"row": to}, device_id_type=MESH)
        copy.start()
        fin_copies.append(copy)
    o_ref[part(row), :] = total
    for k in range(1, rows):
        q = lax.rem(row + k, rows)
        pltpu.make_async_remote_copy(
            src_ref=fin.at[q], dst_ref=fin.at[q], send_sem=fin_out.at[k], recv_sem=fin_got.at[q],
            device_id={"row": q}, device_id_type=MESH).wait_recv()
        o_ref[part(q), :] = fin[q]

    for copy in sent + red_copies + fin_copies:
        copy.wait_send()


def per_device(rows, amplitudes, ladder_ints, tile_mask):
    return pl.pallas_call(
        functools.partial(kernel, rows),
        out_shape=jax.ShapeDtypeStruct((64, 256), jnp.float32),
        in_specs=[pl.BlockSpec(memory_space=pl.ANY)] * 3,
        out_specs=pl.BlockSpec(memory_space=pltpu.VMEM),
        scratch_shapes=[
            pltpu.VMEM((64, 1024), jnp.float32),
            pltpu.VMEM((64, 256), jnp.int32),
            pltpu.VMEM((8, 256), jnp.int32),
            pltpu.SMEM((8, 256), jnp.int32),
            pltpu.VMEM((16, LIVE * TILE, 256), jnp.bfloat16),
            pltpu.VMEM((16, LIVE * TILE, 256), jnp.bfloat16),
            pltpu.VMEM((16, PIECES, 64, WIDTH), jnp.float32),
            pltpu.VMEM((64, 256), jnp.float32),
            pltpu.VMEM((rows, 8, 256), jnp.float32),
            pltpu.VMEM((rows, 8, 256), jnp.float32),
            pltpu.SemaphoreType.DMA((3,)),
            pltpu.SemaphoreType.DMA((16,)),
            pltpu.SemaphoreType.DMA((N_SENT,)),
            pltpu.SemaphoreType.DMA((16 * PIECES,)),
            pltpu.SemaphoreType.DMA((rows,)),
            pltpu.SemaphoreType.DMA((rows,)),
            pltpu.SemaphoreType.DMA((rows,)),
            pltpu.SemaphoreType.DMA((rows,)),
            pltpu.SemaphoreType.REGULAR((ROUNDS,)),
        ] + [pltpu.VMEM((1024, 256), jnp.float32)] * 16,
        compiler_params=pltpu.CompilerParams(
            collective_id=0, has_side_effects=True, vmem_limit_bytes=60 * 1024 * 1024),
    )(amplitudes, ladder_ints, tile_mask.T)


def solution(mesh):
    in_specs = (P(None, ("row", "col")), P("row", "col"), P())
    out_specs = P(None, "col")
    return jax.shard_map(
        functools.partial(per_device, mesh.shape["row"]), mesh=mesh, in_specs=in_specs, out_specs=out_specs,
        check_vma=False)
```

```python
import functools

import jax
import jax.numpy as jnp
from jax import lax
from jax.experimental import pallas as pl
from jax.experimental.pallas import tpu as pltpu
from jax.sharding import PartitionSpec as P

TILE = 64
GROUP = 16
LIVE = 8
PIECES = 2
WIDTH = 256
MESH = pl.DeviceIdType.MESH

TREE = {(0, 1): "xs", (0, 3): "xs", (1, 0): "2s", (0, 2): "s", (1, 1): "s", (1, 3): "s", (1, 2): "s"}
FIRST = ((0, 1), (0, 3), (1, 0))
SECOND = ((1, 1), (1, 3), (1, 2))
ORDER = ((0, 0),) + FIRST + ((0, 2),) + SECOND
N_SENT = (4 + 1 + 3 + 7) * PIECES
ROUNDS = 3


def kernel(rows, t_hbm, v_hbm, m_hbm, o_ref, t_in, m_in, list_v, list_s, v_hi, v_lo, t_all, acc, red, fin,
           in_sem, v_sem, out_sem, got_sem, red_out, red_got, fin_out, fin_got, near_sem, *v_in):
    row = lax.axis_index("row")
    col = lax.axis_index("col")
    core = lax.rem(col, 2)
    z = lax.rem(lax.div(col, 2), 4)
    x_lo = lax.div(col, 8)
    y = lax.div(row, 2)
    x_hi = lax.rem(row, 2)

    def col_of(dx, dz, dc):
        return lax.rem(x_lo + dx, 2) * 8 + lax.rem(z + dz, 4) * 2 + lax.rem(core + dc, 2)

    def row_of(dy, dx):
        return lax.rem(y + dy, 4) * 2 + lax.rem(x_hi + dx, 2)

    link = {"u": col_of(0, 1, 0), "d": col_of(0, 3, 0), "2": col_of(0, 2, 0), "x": col_of(1, 0, 0),
            "s": col_of(0, 0, 1)}
    near = ({"row": row_of(1, 0)}, {"row": row_of(3, 0)}, {"col": link["x"]}, {"row": row_of(0, 1), "col": link["x"]})

    mask_copy = pltpu.make_async_copy(
        m_hbm.at[:, pl.ds(pl.multiple_of(row * 256, 256), 256)], m_in, in_sem.at[0])
    mask_copy.start()
    t_copy = pltpu.make_async_copy(t_hbm, t_in, in_sem.at[1])
    t_copy.start()

    barrier = pltpu.get_barrier_semaphore()
    for to in [{"col": link[way]} for way in "ud2s"] + list(near):
        pl.semaphore_signal(barrier, inc=1, device_id=to, device_id_type=MESH)

    owner = {(e, dc): col_of(e[0], (4 - e[1]) % 4, dc) for e in ORDER for dc in (0, 1)}
    v_of = dict(zip(owner, v_in))
    v_copies = {}
    for n, at in enumerate(owner):
        v_copies[at] = pltpu.make_async_copy(
            v_hbm.at[pl.ds(pl.multiple_of(owner[at] * 1024, 1024), 1024), :], v_of[at], v_sem.at[n])
        v_copies[at].start()

    mask_copy.wait()
    live = jnp.broadcast_to(jnp.max(m_in[...], axis=0, keepdims=True), (8, 256))
    lane = lax.broadcasted_iota(jnp.int32, (8, 256), 1)
    slot = lax.broadcasted_iota(jnp.int32, (8, 256), 0)
    tile = lane & 15
    count = live
    for s in (1, 2, 4, 8):
        count = count + jnp.where(tile >= s, pltpu.roll(count, s, 1), 0)
    place = jnp.where(live > 0, count - 1, 15 - tile + count)
    mine = m_in[pl.ds(pl.multiple_of(lax.div(col, 2) * 8, 8), 8), :]
    bit = slot - lax.rem(col, 2) * 4
    weight = jnp.where(bit == 0, 16, jnp.where(bit == 1, 32, jnp.where(bit == 2, 64, jnp.where(bit == 3, 128, 0))))
    code = jnp.sum(mine * weight, axis=0, keepdims=True)
    entry = jnp.where(place == slot, tile + code, 0)
    for s in (1, 2, 4, 8):
        entry = entry + pltpu.roll(entry, 256 - s, 1)
    list_v[...] = entry
    list_copy = pltpu.make_async_copy(list_v, list_s, in_sem.at[2])
    list_copy.start()
    own = jnp.broadcast_to(pltpu.roll(entry, lax.rem(256 - col * GROUP, 256), 1)[:, :1], (8, 128)) & 15
    t_copy.wait()

    left = lax.broadcasted_iota(jnp.int32, (64, 128), 1) < TILE
    for p in range(LIVE // 2):
        halves = []
        for h in (0, 1):
            at = own[2 * p + h:2 * p + h + 1]
            block = t_in[:, 7 * 128:]
            for b in range(p, 7):
                block = jnp.where(at >> 1 == b, t_in[:, b * 128:(b + 1) * 128], block)
            halves.append(jnp.where(at & 1 != h, pltpu.roll(block, TILE, 1), block))
        t_all[col, p // 2, :, (p % 2) * 128:(p % 2) * 128 + 128] = jnp.where(left, halves[0], halves[1])

    pl.semaphore_wait(barrier, 8)

    sent = []

    def piece(s, p, to, n):
        return pltpu.make_async_remote_copy(
            src_ref=t_all.at[s, p], dst_ref=t_all.at[s, p], send_sem=out_sem.at[n],
            recv_sem=got_sem.at[s * PIECES + p], device_id={"col": to}, device_id_type=MESH)

    def send(s, p, ways):
        for way in ways:
            copy = piece(s, p, link[way], len(sent))
            copy.start()
            sent.append(copy)

    def arrive(e, dc, p):
        piece(owner[e, dc], p, link["s"], 0).wait_recv()

    for p in range(PIECES):
        send(col, p, "udx")
    for p in range(PIECES):
        send(col, p, "s")

    def tell(n):
        for to in near:
            pl.semaphore_signal(near_sem.at[n], inc=1, device_id=to, device_id_type=MESH)

    def hear(n):
        pl.semaphore_wait(near_sem.at[n], len(near))

    tell(0)

    bits = 16 << lax.div(lax.broadcasted_iota(jnp.int32, (1, 256), 1), TILE)

    def prepare(e, dc):
        s = owner[e, dc]
        v_copies[e, dc].wait()

        def one(k, carry):
            at = list_s[k, s * GROUP]
            tile_rows = v_of[e, dc][pl.ds((at & 15) * TILE, TILE), :]
            tile_rows = jnp.where((jnp.full((1, 256), at, jnp.int32) & bits) != 0, tile_rows, 0.0)
            high = tile_rows.astype(jnp.bfloat16)
            low = (tile_rows - high.astype(jnp.float32)).astype(jnp.bfloat16)
            to = pl.ds(pl.multiple_of(k * TILE, TILE), TILE)
            v_hi[s, to, :] = high
            v_lo[s, to, :] = low
            return carry

        lax.fori_loop(0, LIVE, one, 0)

    def multiply(e, dc):
        s = owner[e, dc]
        t = jnp.concatenate([t_all[s, p] for p in range(PIECES)], axis=1)
        high = t.astype(jnp.bfloat16)
        low = (t - high.astype(jnp.float32)).astype(jnp.bfloat16)
        both = jnp.dot(jnp.concatenate([high, low], axis=0), v_hi[s], preferred_element_type=jnp.float32)
        more = jnp.dot(high, v_lo[s], preferred_element_type=jnp.float32)
        acc[...] += both[:64] + (both[64:] + more)

    def pass_on(e, p):
        arrive(e, 0, p)
        send(owner[e, 0], p, TREE[e])

    def sibling(e):
        for p in range(PIECES):
            arrive(e, 1, p)
        multiply(e, 1)

    acc[...] = jnp.zeros_like(acc)
    list_copy.wait()
    prepare((0, 0), 0)
    prepare((0, 0), 1)
    multiply((0, 0), 0)
    sibling((0, 0))
    for e in FIRST:
        prepare(e, 0)
        prepare(e, 1)
    hear(0)
    tell(1)
    for p in range(PIECES):
        for e in FIRST:
            arrive(e, 0, p)
            if e != (1, 0):
                send(owner[e, 0], p, "x")
        send(col, p, "2")
        send(owner[(1, 0), 0], p, "2")
        for e in FIRST:
            send(owner[e, 0], p, "s")
    for e in ((0, 2),) + SECOND[:2]:
        prepare(e, 0)
        prepare(e, 1)
    for p in range(PIECES):
        pass_on((0, 2), p)
    hear(1)
    tell(2)
    for e in FIRST:
        multiply(e, 0)
    for e in SECOND[2:]:
        prepare(e, 0)
        prepare(e, 1)
    for e in FIRST:
        sibling(e)
    multiply((0, 2), 0)
    hear(2)
    for p in range(PIECES):
        for e in SECOND:
            pass_on(e, p)
    sibling((0, 2))
    for e in SECOND:
        multiply(e, 0)
    for e in SECOND:
        sibling(e)

    def part(q):
        return pl.ds(pl.multiple_of(q * 8, 8), 8)

    red_copies, fin_copies = [], []
    for k in range(1, rows):
        to = lax.rem(row + k, rows)
        copy = pltpu.make_async_remote_copy(
            src_ref=acc.at[part(to)], dst_ref=red.at[k], send_sem=red_out.at[k], recv_sem=red_got.at[k],
            device_id={"row": to}, device_id_type=MESH)
        copy.start()
        red_copies.append(copy)
    total = acc[part(row), :]
    for copy in red_copies:
        copy.wait_recv()
    for k in range(1, rows):
        total = total + red[k]
    fin[row] = total
    for k in range(1, rows):
        to = lax.rem(row + k, rows)
        copy = pltpu.make_async_remote_copy(
            src_ref=fin.at[row], dst_ref=fin.at[row], send_sem=fin_out.at[k], recv_sem=fin_got.at[row],
            device_id={"row": to}, device_id_type=MESH)
        copy.start()
        fin_copies.append(copy)
    o_ref[part(row), :] = total
    for k in range(1, rows):
        q = lax.rem(row + k, rows)
        pltpu.make_async_remote_copy(
            src_ref=fin.at[q], dst_ref=fin.at[q], send_sem=fin_out.at[k], recv_sem=fin_got.at[q],
            device_id={"row": q}, device_id_type=MESH).wait_recv()
        o_ref[part(q), :] = fin[q]

    for copy in sent + red_copies + fin_copies:
        copy.wait_send()


def per_device(rows, amplitudes, ladder_ints, tile_mask):
    return pl.pallas_call(
        functools.partial(kernel, rows),
        out_shape=jax.ShapeDtypeStruct((64, 256), jnp.float32),
        in_specs=[pl.BlockSpec(memory_space=pl.ANY)] * 3,
        out_specs=pl.BlockSpec(memory_space=pltpu.VMEM),
        scratch_shapes=[
            pltpu.VMEM((64, 1024), jnp.float32),
            pltpu.VMEM((64, 256), jnp.int32),
            pltpu.VMEM((8, 256), jnp.int32),
            pltpu.SMEM((8, 256), jnp.int32),
            pltpu.VMEM((16, LIVE * TILE, 256), jnp.bfloat16),
            pltpu.VMEM((16, LIVE * TILE, 256), jnp.bfloat16),
            pltpu.VMEM((16, PIECES, 64, WIDTH), jnp.float32),
            pltpu.VMEM((64, 256), jnp.float32),
            pltpu.VMEM((rows, 8, 256), jnp.float32),
            pltpu.VMEM((rows, 8, 256), jnp.float32),
            pltpu.SemaphoreType.DMA((3,)),
            pltpu.SemaphoreType.DMA((16,)),
            pltpu.SemaphoreType.DMA((N_SENT,)),
            pltpu.SemaphoreType.DMA((16 * PIECES,)),
            pltpu.SemaphoreType.DMA((rows,)),
            pltpu.SemaphoreType.DMA((rows,)),
            pltpu.SemaphoreType.DMA((rows,)),
            pltpu.SemaphoreType.DMA((rows,)),
            pltpu.SemaphoreType.REGULAR((ROUNDS,)),
        ] + [pltpu.VMEM((1024, 256), jnp.float32)] * 16,
        compiler_params=pltpu.CompilerParams(
            collective_id=0, has_side_effects=True, vmem_limit_bytes=60 * 1024 * 1024),
    )(amplitudes, ladder_ints, tile_mask.T)


def solution(mesh):
    in_specs = (P(None, ("row", "col")), P("row", "col"), P())
    out_specs = P(None, "col")
    return jax.shard_map(
        functools.partial(per_device, mesh.shape["row"]), mesh=mesh, in_specs=in_specs, out_specs=out_specs,
        check_vma=False)
```

```python
import functools

import jax
import jax.numpy as jnp
from jax import lax
from jax.experimental import pallas as pl
from jax.experimental.pallas import tpu as pltpu
from jax.sharding import PartitionSpec as P

TILE = 64
GROUP = 16
LIVE = 8
PIECES = 2
ROWS = (0, 24, 64)
MESH = pl.DeviceIdType.MESH

TREES = ({(0, 0): "udx", (0, 1): "xu", (0, 3): "x", (1, 0): "2"}, {(0, 0): "udx", (0, 3): "xd", (1, 0): "u2"})
FIRST = ((0, 1), (0, 3), (1, 0))
SECOND = ((1, 1), (1, 3), (1, 2))
LATE = ((0, 2), (1, 1), (1, 3), (1, 2))
ORDER = ((0, 0),) + FIRST + LATE
N_SENT = 15 * PIECES
ROUNDS = 3


def kernel(rows, t_hbm, v_hbm, m_hbm, o_ref, t_in, m_in, list_v, list_s, v_hi, v_lo, t_all, acc, red,
           in_sem, v_sem, out_sem, got_sem, red_out, red_got, near_sem, *v_in):
    row = lax.axis_index("row")
    col = lax.axis_index("col")
    core = lax.rem(col, 2)
    z = lax.rem(lax.div(col, 2), 4)
    x_lo = lax.div(col, 8)
    y = lax.div(row, 2)
    x_hi = lax.rem(row, 2)

    def col_of(dx, dz, dc):
        return lax.rem(x_lo + dx, 2) * 8 + lax.rem(z + dz, 4) * 2 + lax.rem(core + dc, 2)

    def row_of(dy, dx):
        return lax.rem(y + dy, 4) * 2 + lax.rem(x_hi + dx, 2)

    link = {"u": col_of(0, 1, 0), "d": col_of(0, 3, 0), "2": col_of(0, 2, 0), "x": col_of(1, 0, 0),
            "s": col_of(0, 0, 1)}
    near = ({"row": row_of(1, 0)}, {"row": row_of(3, 0)}, {"col": link["x"]}, {"row": row_of(0, 1), "col": link["x"]})

    mask_copy = pltpu.make_async_copy(
        m_hbm.at[:, pl.ds(pl.multiple_of(row * 256, 256), 256)], m_in, in_sem.at[0])
    mask_copy.start()
    t_copy = pltpu.make_async_copy(t_hbm, t_in, in_sem.at[1])
    t_copy.start()

    barrier = pltpu.get_barrier_semaphore()
    for to in [{"col": link[way]} for way in "ud2s"] + list(near):
        pl.semaphore_signal(barrier, inc=1, device_id=to, device_id_type=MESH)

    owner = {(e, dc): col_of(e[0], (4 - e[1]) % 4, dc) for e in ORDER for dc in (0, 1)}
    v_of = dict(zip(owner, v_in))
    v_copies = {}
    for n, at in enumerate(owner):
        v_copies[at] = pltpu.make_async_copy(
            v_hbm.at[pl.ds(pl.multiple_of(owner[at] * 1024, 1024), 1024), :], v_of[at], v_sem.at[n])
        v_copies[at].start()

    mask_copy.wait()
    live = jnp.broadcast_to(jnp.max(m_in[...], axis=0, keepdims=True), (8, 256))
    lane = lax.broadcasted_iota(jnp.int32, (8, 256), 1)
    slot = lax.broadcasted_iota(jnp.int32, (8, 256), 0)
    tile = lane & 15
    count = live
    for s in (1, 2, 4, 8):
        count = count + jnp.where(tile >= s, pltpu.roll(count, s, 1), 0)
    place = jnp.where(live > 0, count - 1, 15 - tile + count)
    mine = m_in[pl.ds(pl.multiple_of(lax.div(col, 2) * 8, 8), 8), :]
    bit = slot - lax.rem(col, 2) * 4
    weight = jnp.where(bit == 0, 16, jnp.where(bit == 1, 32, jnp.where(bit == 2, 64, jnp.where(bit == 3, 128, 0))))
    code = jnp.sum(mine * weight, axis=0, keepdims=True)
    entry = jnp.where(place == slot, tile + code, 0)
    for s in (1, 2, 4, 8):
        entry = entry + pltpu.roll(entry, 256 - s, 1)
    list_v[...] = entry
    list_copy = pltpu.make_async_copy(list_v, list_s, in_sem.at[2])
    list_copy.start()
    own = jnp.broadcast_to(pltpu.roll(entry, lax.rem(256 - col * GROUP, 256), 1)[:, :1], (8, 128)) & 15
    t_copy.wait()

    left = lax.broadcasted_iota(jnp.int32, (64, 128), 1) < TILE
    for p in range(LIVE // 2):
        halves = []
        for h in (0, 1):
            at = own[2 * p + h:2 * p + h + 1]
            block = t_in[:, 7 * 128:]
            for b in range(p, 7):
                block = jnp.where(at >> 1 == b, t_in[:, b * 128:(b + 1) * 128], block)
            halves.append(jnp.where(at & 1 != h, pltpu.roll(block, TILE, 1), block))
        t_all[col, :, p * 128:p * 128 + 128] = jnp.where(left, halves[0], halves[1])

    pl.semaphore_wait(barrier, 8)

    sent = []

    def part(p):
        return pl.ds(ROWS[p], ROWS[p + 1] - ROWS[p])

    def piece(s, p, to, n):
        return pltpu.make_async_remote_copy(
            src_ref=t_all.at[s, part(p)], dst_ref=t_all.at[s, part(p)], send_sem=out_sem.at[n],
            recv_sem=got_sem.at[s * PIECES + p], device_id={"col": to}, device_id_type=MESH)

    def send(s, p, ways):
        for way in ways:
            copy = piece(s, p, link[way], len(sent))
            copy.start()
            sent.append(copy)

    def arrive(e, dc, p):
        piece(owner[e, dc], p, link["s"], 0).wait_recv()

    def ways(e, p, which):
        return "".join(w for w in TREES[p % len(TREES)].get(e, "") if w in which)

    for p in range(PIECES):
        send(col, p, "udx")
    for p in range(PIECES):
        send(col, p, "s")

    def tell(n):
        for to in near:
            pl.semaphore_signal(near_sem.at[n], inc=1, device_id=to, device_id_type=MESH)

    def hear(n):
        pl.semaphore_wait(near_sem.at[n], len(near))

    tell(0)

    bits = 16 << lax.div(lax.broadcasted_iota(jnp.int32, (1, 256), 1), TILE)

    def prepare(e, dc):
        s = owner[e, dc]
        v_copies[e, dc].wait()

        def one(k, carry):
            at = list_s[k, s * GROUP]
            tile_rows = v_of[e, dc][pl.ds((at & 15) * TILE, TILE), :]
            tile_rows = jnp.where((jnp.full((1, 256), at, jnp.int32) & bits) != 0, tile_rows, 0.0)
            high = tile_rows.astype(jnp.bfloat16)
            low = (tile_rows - high.astype(jnp.float32)).astype(jnp.bfloat16)
            to = pl.ds(pl.multiple_of(k * TILE, TILE), TILE)
            v_hi[s, to, :] = high
            v_lo[s, to, :] = low
            return carry

        lax.fori_loop(0, LIVE, one, 0)

    def multiply(e, dc, p):
        s = owner[e, dc]
        t = t_all[s, part(p), :]
        high = t.astype(jnp.bfloat16)
        low = (t - high.astype(jnp.float32)).astype(jnp.bfloat16)
        both = jnp.dot(jnp.concatenate([high, low], axis=0), v_hi[s], preferred_element_type=jnp.float32)
        more = jnp.dot(high, v_lo[s], preferred_element_type=jnp.float32)
        n = t.shape[0]
        acc[part(p), :] += both[:n] + (both[n:] + more)

    def pass_on(e, p):
        arrive(e, 0, p)
        send(owner[e, 0], p, ways(e, p, "ud") + "s")

    def sibling(e, p):
        arrive(e, 1, p)
        multiply(e, 1, p)

    acc[...] = jnp.zeros_like(acc)
    list_copy.wait()
    prepare((0, 0), 0)
    prepare((0, 0), 1)
    for p in range(PIECES):
        multiply((0, 0), 0, p)
    for p in range(PIECES):
        sibling((0, 0), p)
    for e in FIRST:
        prepare(e, 0)
        prepare(e, 1)
    hear(0)
    tell(1)
    for p in range(PIECES):
        for e in FIRST:
            arrive(e, 0, p)
            send(owner[e, 0], p, ways(e, p, "x"))
            send(owner[e, 0], p, ways(e, p, "ud"))
        send(col, p, ways((0, 0), p, "2"))
        send(owner[(1, 0), 0], p, ways((1, 0), p, "2"))
        for e in FIRST:
            send(owner[e, 0], p, "s")
    for e in LATE:
        prepare(e, 0)
        prepare(e, 1)
    hear(1)
    tell(2)
    for e in FIRST:
        multiply(e, 0, 0)
    for e in FIRST:
        sibling(e, 0)
    hear(2)

    red_copies = []

    def add_up(k, q, p):
        return pltpu.make_async_remote_copy(
            src_ref=acc.at[part(p)], dst_ref=red.at[q, part(p)], send_sem=red_out.at[p, k], recv_sem=red_got.at[p, q],
            device_id={"row": lax.rem(row + k, rows)}, device_id_type=MESH)

    for p in range(PIECES):
        for e in LATE:
            pass_on(e, p)
        if p > 0:
            for e in FIRST:
                multiply(e, 0, p)
            for e in FIRST:
                sibling(e, p)
        for e in LATE:
            multiply(e, 0, p)
        for e in LATE:
            sibling(e, p)
        for k in range(1, rows):
            copy = add_up(k, row, p)
            copy.start()
            red_copies.append(copy)
        red[row, part(p), :] = acc[part(p), :]
    for p in range(PIECES):
        for k in range(1, rows):
            add_up(k, lax.rem(row + k, rows), p).wait_recv()
        total = red[0, part(p), :]
        for q in range(1, rows):
            total = total + red[q, part(p), :]
        o_ref[part(p), :] = total
    for copy in sent + red_copies:
        copy.wait_send()


def per_device(rows, amplitudes, ladder_ints, tile_mask):
    return pl.pallas_call(
        functools.partial(kernel, rows),
        out_shape=jax.ShapeDtypeStruct((64, 256), jnp.float32),
        in_specs=[pl.BlockSpec(memory_space=pl.ANY)] * 3,
        out_specs=pl.BlockSpec(memory_space=pltpu.VMEM),
        scratch_shapes=[
            pltpu.VMEM((64, 1024), jnp.float32),
            pltpu.VMEM((64, 256), jnp.int32),
            pltpu.VMEM((8, 256), jnp.int32),
            pltpu.SMEM((8, 256), jnp.int32),
            pltpu.VMEM((16, LIVE * TILE, 256), jnp.bfloat16),
            pltpu.VMEM((16, LIVE * TILE, 256), jnp.bfloat16),
            pltpu.VMEM((16, 64, 512), jnp.float32),
            pltpu.VMEM((64, 256), jnp.float32),
            pltpu.VMEM((rows, 64, 256), jnp.float32),
            pltpu.SemaphoreType.DMA((3,)),
            pltpu.SemaphoreType.DMA((16,)),
            pltpu.SemaphoreType.DMA((N_SENT,)),
            pltpu.SemaphoreType.DMA((16 * PIECES,)),
            pltpu.SemaphoreType.DMA((PIECES, rows)),
            pltpu.SemaphoreType.DMA((PIECES, rows)),
            pltpu.SemaphoreType.REGULAR((ROUNDS,)),
        ] + [pltpu.VMEM((1024, 256), jnp.float32)] * 16,
        compiler_params=pltpu.CompilerParams(
            collective_id=0, has_side_effects=True, vmem_limit_bytes=60 * 1024 * 1024),
    )(amplitudes, ladder_ints, tile_mask.T)


def solution(mesh):
    in_specs = (P(None, ("row", "col")), P("row", "col"), P())
    out_specs = P(None, "col")
    return jax.shard_map(
        functools.partial(per_device, mesh.shape["row"]), mesh=mesh, in_specs=in_specs, out_specs=out_specs,
        check_vma=False)
```

```python
import functools

import jax
import jax.numpy as jnp
from jax import lax
from jax.experimental import pallas as pl
from jax.experimental.pallas import tpu as pltpu
from jax.sharding import PartitionSpec as P

TILE = 64
GROUP = 16
LIVE = 8
PIECES = 2
ROWS = (0, 32, 64)
MESH = pl.DeviceIdType.MESH

TREES = ({(0, 0): "udx", (0, 1): "xu", (0, 3): "x", (1, 0): "2"}, {(0, 0): "udx", (0, 3): "xd", (1, 0): "u2"})
FIRST = ((0, 1), (0, 3), (1, 0))
SECOND = ((1, 1), (1, 3), (1, 2))
LATE = ((0, 2), (1, 1), (1, 3), (1, 2))
ORDER = ((0, 0),) + FIRST + LATE
N_SENT = 15 * PIECES
ROUNDS = 3


def kernel(rows, t_hbm, v_hbm, m_hbm, o_ref, t_in, m_in, list_v, list_s, v_hi, v_lo, t_all, acc, sum_y, sum_x, sum_all,
           in_sem, v_sem, out_sem, got_sem, y_out, y_got, x_out, x_got, all_out, all_got, near_sem, *v_in):
    row = lax.axis_index("row")
    col = lax.axis_index("col")
    core = lax.rem(col, 2)
    z = lax.rem(lax.div(col, 2), 4)
    x_lo = lax.div(col, 8)
    y = lax.div(row, 2)
    x_hi = lax.rem(row, 2)

    def col_of(dx, dz, dc):
        return lax.rem(x_lo + dx, 2) * 8 + lax.rem(z + dz, 4) * 2 + lax.rem(core + dc, 2)

    def row_of(dy, dx):
        return lax.rem(y + dy, 4) * 2 + lax.rem(x_hi + dx, 2)

    link = {"u": col_of(0, 1, 0), "d": col_of(0, 3, 0), "2": col_of(0, 2, 0), "x": col_of(1, 0, 0),
            "s": col_of(0, 0, 1)}
    near = ({"row": row_of(1, 0)}, {"row": row_of(3, 0)}, {"col": link["x"]}, {"row": row_of(0, 1), "col": link["x"]})

    mask_copy = pltpu.make_async_copy(
        m_hbm.at[:, pl.ds(pl.multiple_of(row * 256, 256), 256)], m_in, in_sem.at[0])
    mask_copy.start()
    t_copy = pltpu.make_async_copy(t_hbm, t_in, in_sem.at[1])
    t_copy.start()

    barrier = pltpu.get_barrier_semaphore()
    for to in [{"col": link[way]} for way in "ud2s"] + list(near):
        pl.semaphore_signal(barrier, inc=1, device_id=to, device_id_type=MESH)

    owner = {(e, dc): col_of(e[0], (4 - e[1]) % 4, dc) for e in ORDER for dc in (0, 1)}
    v_of = dict(zip(owner, v_in))
    v_copies = {}
    for n, at in enumerate(owner):
        v_copies[at] = pltpu.make_async_copy(
            v_hbm.at[pl.ds(pl.multiple_of(owner[at] * 1024, 1024), 1024), :], v_of[at], v_sem.at[n])
        v_copies[at].start()

    mask_copy.wait()
    live = jnp.broadcast_to(jnp.max(m_in[...], axis=0, keepdims=True), (8, 256))
    lane = lax.broadcasted_iota(jnp.int32, (8, 256), 1)
    slot = lax.broadcasted_iota(jnp.int32, (8, 256), 0)
    tile = lane & 15
    count = live
    for s in (1, 2, 4, 8):
        count = count + jnp.where(tile >= s, pltpu.roll(count, s, 1), 0)
    place = jnp.where(live > 0, count - 1, 15 - tile + count)
    mine = m_in[pl.ds(pl.multiple_of(lax.div(col, 2) * 8, 8), 8), :]
    bit = slot - lax.rem(col, 2) * 4
    weight = jnp.where(bit == 0, 16, jnp.where(bit == 1, 32, jnp.where(bit == 2, 64, jnp.where(bit == 3, 128, 0))))
    code = jnp.sum(mine * weight, axis=0, keepdims=True)
    entry = jnp.where(place == slot, tile + code, 0)
    for s in (1, 2, 4, 8):
        entry = entry + pltpu.roll(entry, 256 - s, 1)
    list_v[...] = entry
    list_copy = pltpu.make_async_copy(list_v, list_s, in_sem.at[2])
    list_copy.start()
    own = jnp.broadcast_to(pltpu.roll(entry, lax.rem(256 - col * GROUP, 256), 1)[:, :1], (8, 128)) & 15
    t_copy.wait()

    sent = []

    def part(p):
        return pl.ds(ROWS[p], ROWS[p + 1] - ROWS[p])

    left = lax.broadcasted_iota(jnp.int32, (1, 128), 1) < TILE

    def pack(p):
        for n in range(LIVE // 2):
            halves = []
            for h in (0, 1):
                at = own[2 * n + h:2 * n + h + 1]
                block = t_in[part(p), 7 * 128:]
                for b in range(n, 7):
                    block = jnp.where(at >> 1 == b, t_in[part(p), b * 128:(b + 1) * 128], block)
                halves.append(jnp.where(at & 1 != h, pltpu.roll(block, TILE, 1), block))
            t_all[col, part(p), n * 128:n * 128 + 128] = jnp.where(left, halves[0], halves[1])

    def piece(s, p, to, n):
        return pltpu.make_async_remote_copy(
            src_ref=t_all.at[s, part(p)], dst_ref=t_all.at[s, part(p)], send_sem=out_sem.at[n],
            recv_sem=got_sem.at[s * PIECES + p], device_id={"col": to}, device_id_type=MESH)

    def send(s, p, ways):
        for way in ways:
            copy = piece(s, p, link[way], len(sent))
            copy.start()
            sent.append(copy)

    def arrive(e, dc, p):
        piece(owner[e, dc], p, link["s"], 0).wait_recv()

    def ways(e, p, which):
        return "".join(w for w in TREES[p % len(TREES)].get(e, "") if w in which)

    pack(0)
    pl.semaphore_wait(barrier, 8)
    send(col, 0, "udx")
    pack(1)
    send(col, 1, "udx")
    for p in range(PIECES):
        send(col, p, "s")

    def tell(n):
        for to in near:
            pl.semaphore_signal(near_sem.at[n], inc=1, device_id=to, device_id_type=MESH)

    def hear(n):
        pl.semaphore_wait(near_sem.at[n], len(near))

    tell(0)

    bits = 16 << lax.div(lax.broadcasted_iota(jnp.int32, (1, 256), 1), TILE)

    def prepare(e, dc):
        s = owner[e, dc]
        v_copies[e, dc].wait()

        def one(k, carry):
            at = list_s[k, s * GROUP]
            tile_rows = v_of[e, dc][pl.ds((at & 15) * TILE, TILE), :]
            tile_rows = jnp.where((jnp.full((1, 256), at, jnp.int32) & bits) != 0, tile_rows, 0.0)
            high = tile_rows.astype(jnp.bfloat16)
            low = (tile_rows - high.astype(jnp.float32)).astype(jnp.bfloat16)
            to = pl.ds(pl.multiple_of(k * TILE, TILE), TILE)
            v_hi[s, to, :] = high
            v_lo[s, to, :] = low
            return carry

        lax.fori_loop(0, LIVE, one, 0)

    def multiply(e, dc, p):
        s = owner[e, dc]
        t = t_all[s, part(p), :]
        high = t.astype(jnp.bfloat16)
        low = (t - high.astype(jnp.float32)).astype(jnp.bfloat16)
        both = jnp.dot(jnp.concatenate([high, low], axis=0), v_hi[s], preferred_element_type=jnp.float32)
        more = jnp.dot(high, v_lo[s], preferred_element_type=jnp.float32)
        n = t.shape[0]
        acc[part(p), :] += both[:n] + (both[n:] + more)

    def pass_on(e, p):
        arrive(e, 0, p)
        send(owner[e, 0], p, ways(e, p, "ud") + "s")

    def sibling(e, p):
        arrive(e, 1, p)
        multiply(e, 1, p)

    acc[...] = jnp.zeros_like(acc)
    list_copy.wait()
    prepare((0, 0), 0)
    prepare((0, 0), 1)
    for p in range(PIECES):
        multiply((0, 0), 0, p)
    for p in range(PIECES):
        sibling((0, 0), p)
    for e in FIRST:
        prepare(e, 0)
        prepare(e, 1)
    hear(0)
    tell(1)
    for p in range(PIECES):
        for e in FIRST:
            arrive(e, 0, p)
            send(owner[e, 0], p, ways(e, p, "x"))
            send(owner[e, 0], p, ways(e, p, "ud"))
        send(owner[(1, 0), 0], p, ways((1, 0), p, "2"))
        for e in FIRST:
            send(owner[e, 0], p, "s")
    for e in LATE:
        prepare(e, 0)
        prepare(e, 1)
    hear(1)
    tell(2)
    for e in FIRST:
        multiply(e, 0, 0)
    for e in FIRST:
        sibling(e, 0)
    hear(2)

    def over_y(k, at, q):
        return pltpu.make_async_remote_copy(
            src_ref=acc.at[part(0)], dst_ref=sum_y.at[at], send_sem=y_out.at[k], recv_sem=y_got.at[at],
            device_id={"row": q}, device_id_type=MESH)

    def over_x(at):
        return pltpu.make_async_remote_copy(
            src_ref=sum_x.at[at], dst_ref=sum_x.at[at], send_sem=x_out.at[0], recv_sem=x_got.at[at],
            device_id={"row": row_of(0, 1)}, device_id_type=MESH)

    def over_all(k, at, q):
        return pltpu.make_async_remote_copy(
            src_ref=acc.at[part(1)], dst_ref=sum_all.at[at], send_sem=all_out.at[k], recv_sem=all_got.at[at],
            device_id={"row": q}, device_id_type=MESH)

    sums = [over_y(k, y, row_of(k, 0)) for k in range(1, 4)]
    for e in LATE:
        pass_on(e, 0)
    for e in LATE:
        multiply(e, 0, 0)
    for e in LATE:
        sibling(e, 0)
    for copy in sums:
        copy.start()
    sum_y[y] = acc[part(0), :]
    for e in LATE:
        pass_on(e, 1)
    for e in FIRST:
        multiply(e, 0, 1)
    for e in FIRST:
        sibling(e, 1)
    for e in LATE:
        multiply(e, 0, 1)
    for e in LATE:
        sibling(e, 1)
    far = ((2, 1), (1, 1), (3, 1), (2, 0), (0, 1), (1, 0), (3, 0))
    last = [over_all(k, row, row_of(*far[k - 1])) for k in range(1, rows)]
    for copy in last:
        copy.start()
    sum_all[row] = acc[part(1), :]
    for copy in sent + sums:
        copy.wait_send()

    for k in range(1, 4):
        over_y(k, lax.rem(y + k, 4), row_of(k, 0)).wait_recv()
    sum_x[x_hi] = (sum_y[0] + sum_y[1]) + (sum_y[2] + sum_y[3])
    across = over_x(x_hi)
    across.start()
    for copy in last:
        copy.wait_send()
    for k in range(1, rows):
        q = lax.rem(row + k, rows)
        over_all(k, q, q).wait_recv()
    total = sum_all[0]
    for q in range(1, rows):
        total = total + sum_all[q]
    o_ref[part(1), :] = total
    over_x(1 - x_hi).wait_recv()
    o_ref[part(0), :] = sum_x[0] + sum_x[1]
    copy = across
    copy.wait_send()


def per_device(rows, amplitudes, ladder_ints, tile_mask):
    return pl.pallas_call(
        functools.partial(kernel, rows),
        out_shape=jax.ShapeDtypeStruct((64, 256), jnp.float32),
        in_specs=[pl.BlockSpec(memory_space=pl.ANY)] * 3,
        out_specs=pl.BlockSpec(memory_space=pltpu.VMEM),
        scratch_shapes=[
            pltpu.VMEM((64, 1024), jnp.float32),
            pltpu.VMEM((64, 256), jnp.int32),
            pltpu.VMEM((8, 256), jnp.int32),
            pltpu.SMEM((8, 256), jnp.int32),
            pltpu.VMEM((16, LIVE * TILE, 256), jnp.bfloat16),
            pltpu.VMEM((16, LIVE * TILE, 256), jnp.bfloat16),
            pltpu.VMEM((16, 64, 512), jnp.float32),
            pltpu.VMEM((64, 256), jnp.float32),
            pltpu.VMEM((4, ROWS[1], 256), jnp.float32),
            pltpu.VMEM((2, ROWS[1], 256), jnp.float32),
            pltpu.VMEM((rows, 64 - ROWS[1], 256), jnp.float32),
            pltpu.SemaphoreType.DMA((3,)),
            pltpu.SemaphoreType.DMA((16,)),
            pltpu.SemaphoreType.DMA((N_SENT,)),
            pltpu.SemaphoreType.DMA((16 * PIECES,)),
            pltpu.SemaphoreType.DMA((4,)),
            pltpu.SemaphoreType.DMA((4,)),
            pltpu.SemaphoreType.DMA((1,)),
            pltpu.SemaphoreType.DMA((2,)),
            pltpu.SemaphoreType.DMA((rows,)),
            pltpu.SemaphoreType.DMA((rows,)),
            pltpu.SemaphoreType.REGULAR((ROUNDS,)),
        ] + [pltpu.VMEM((1024, 256), jnp.float32)] * 16,
        compiler_params=pltpu.CompilerParams(
            collective_id=0, has_side_effects=True, vmem_limit_bytes=60 * 1024 * 1024),
    )(amplitudes, ladder_ints, tile_mask.T)


def solution(mesh):
    in_specs = (P(None, ("row", "col")), P("row", "col"), P())
    out_specs = P(None, "col")
    return jax.shard_map(
        functools.partial(per_device, mesh.shape["row"]), mesh=mesh, in_specs=in_specs, out_specs=out_specs,
        check_vma=False)
```

```python
import functools

import jax
import jax.numpy as jnp
from jax import lax
from jax.experimental import pallas as pl
from jax.experimental.pallas import tpu as pltpu
from jax.sharding import PartitionSpec as P

TILE = 64
GROUP = 16
LIVE = 8
PIECES = 2
ROWS = (0, 32, 64)
MESH = pl.DeviceIdType.MESH

TREES = ({(0, 0): "udx", (0, 1): "xu", (0, 3): "x", (1, 0): "2"}, {(0, 0): "udx", (0, 3): "xd", (1, 0): "u2"})
FIRST = ((0, 1), (0, 3), (1, 0))
SECOND = ((1, 1), (1, 3), (1, 2))
LATE = ((0, 2), (1, 1), (1, 3), (1, 2))
ORDER = ((0, 0),) + FIRST + LATE
N_SENT = 15 * PIECES
ROUNDS = 3


def kernel(rows, t_hbm, v_hbm, m_hbm, o_ref, t_in, m_in, list_v, list_s, v_hi, v_lo, t_all, acc, sum_y, sum_x, sum_all,
           in_sem, v_sem, out_sem, got_sem, y_out, y_got, x_out, x_got, all_out, all_got, near_sem, *v_in):
    row = lax.axis_index("row")
    col = lax.axis_index("col")
    core = lax.rem(col, 2)
    z = lax.rem(lax.div(col, 2), 4)
    x_lo = lax.div(col, 8)
    y = lax.div(row, 2)
    x_hi = lax.rem(row, 2)

    def col_of(dx, dz, dc):
        return lax.rem(x_lo + dx, 2) * 8 + lax.rem(z + dz, 4) * 2 + lax.rem(core + dc, 2)

    def row_of(dy, dx):
        return lax.rem(y + dy, 4) * 2 + lax.rem(x_hi + dx, 2)

    link = {"u": col_of(0, 1, 0), "d": col_of(0, 3, 0), "2": col_of(0, 2, 0), "x": col_of(1, 0, 0),
            "s": col_of(0, 0, 1)}
    near = ({"row": row_of(1, 0)}, {"row": row_of(3, 0)}, {"col": link["x"]}, {"row": row_of(0, 1), "col": link["x"]})

    mask_copy = pltpu.make_async_copy(
        m_hbm.at[:, pl.ds(pl.multiple_of(row * 256, 256), 256)], m_in, in_sem.at[0])
    mask_copy.start()
    t_copy = pltpu.make_async_copy(t_hbm, t_in, in_sem.at[1])
    t_copy.start()

    barrier = pltpu.get_barrier_semaphore()
    for to in [{"col": link[way]} for way in "ud2s"] + list(near):
        pl.semaphore_signal(barrier, inc=1, device_id=to, device_id_type=MESH)

    owner = {(e, dc): col_of(e[0], (4 - e[1]) % 4, dc) for e in ORDER for dc in (0, 1)}
    v_of = dict(zip(owner, v_in))
    v_copies = {}
    for n, at in enumerate(owner):
        v_copies[at] = pltpu.make_async_copy(
            v_hbm.at[pl.ds(pl.multiple_of(owner[at] * 1024, 1024), 1024), :], v_of[at], v_sem.at[n])
        v_copies[at].start()

    mask_copy.wait()
    live = jnp.broadcast_to(jnp.max(m_in[...], axis=0, keepdims=True), (8, 256))
    lane = lax.broadcasted_iota(jnp.int32, (8, 256), 1)
    slot = lax.broadcasted_iota(jnp.int32, (8, 256), 0)
    tile = lane & 15
    count = live
    for s in (1, 2, 4, 8):
        count = count + jnp.where(tile >= s, pltpu.roll(count, s, 1), 0)
    place = jnp.where(live > 0, count - 1, 15 - tile + count)
    mine = m_in[pl.ds(pl.multiple_of(lax.div(col, 2) * 8, 8), 8), :]
    bit = slot - lax.rem(col, 2) * 4
    weight = jnp.where(bit == 0, 16, jnp.where(bit == 1, 32, jnp.where(bit == 2, 64, jnp.where(bit == 3, 128, 0))))
    code = jnp.sum(mine * weight, axis=0, keepdims=True)
    entry = jnp.where(place == slot, tile + code, 0)
    for s in (1, 2, 4, 8):
        entry = entry + pltpu.roll(entry, 256 - s, 1)
    list_v[...] = entry
    list_copy = pltpu.make_async_copy(list_v, list_s, in_sem.at[2])
    list_copy.start()
    own = jnp.broadcast_to(pltpu.roll(entry, lax.rem(256 - col * GROUP, 256), 1)[:, :1], (8, 128)) & 15
    t_copy.wait()

    sent = []

    def part(p):
        return pl.ds(ROWS[p], ROWS[p + 1] - ROWS[p])

    left = lax.broadcasted_iota(jnp.int32, (1, 128), 1) < TILE

    def pack(p):
        for n in range(LIVE // 2):
            halves = []
            for h in (0, 1):
                at = own[2 * n + h:2 * n + h + 1]
                block = t_in[part(p), 7 * 128:]
                for b in range(n, 7):
                    block = jnp.where(at >> 1 == b, t_in[part(p), b * 128:(b + 1) * 128], block)
                halves.append(jnp.where(at & 1 != h, pltpu.roll(block, TILE, 1), block))
            t_all[col, part(p), n * 128:n * 128 + 128] = jnp.where(left, halves[0], halves[1])

    def piece(s, p, to, n):
        return pltpu.make_async_remote_copy(
            src_ref=t_all.at[s, part(p)], dst_ref=t_all.at[s, part(p)], send_sem=out_sem.at[n],
            recv_sem=got_sem.at[s * PIECES + p], device_id={"col": to}, device_id_type=MESH)

    def send(s, p, ways):
        for way in ways:
            copy = piece(s, p, link[way], len(sent))
            copy.start()
            sent.append(copy)

    def arrive(e, dc, p):
        piece(owner[e, dc], p, link["s"], 0).wait_recv()

    def ways(e, p, which):
        return "".join(w for w in TREES[p % len(TREES)].get(e, "") if w in which)

    pack(0)
    pl.semaphore_wait(barrier, 8)
    send(col, 0, "udx")
    pack(1)
    send(col, 1, "udx")
    for p in range(PIECES):
        send(col, p, "s")

    def tell(n):
        for to in near:
            pl.semaphore_signal(near_sem.at[n], inc=1, device_id=to, device_id_type=MESH)

    def hear(n):
        pl.semaphore_wait(near_sem.at[n], len(near))

    tell(0)

    bits = 16 << lax.div(lax.broadcasted_iota(jnp.int32, (1, 256), 1), TILE)

    def prepare(e, dc):
        s = owner[e, dc]
        v_copies[e, dc].wait()

        def one(k, carry):
            at = list_s[k, s * GROUP]
            tile_rows = v_of[e, dc][pl.ds((at & 15) * TILE, TILE), :]
            tile_rows = jnp.where((jnp.full((1, 256), at, jnp.int32) & bits) != 0, tile_rows, 0.0)
            high = tile_rows.astype(jnp.bfloat16)
            low = (tile_rows - high.astype(jnp.float32)).astype(jnp.bfloat16)
            to = pl.ds(pl.multiple_of(k * TILE, TILE), TILE)
            v_hi[s, to, :] = high
            v_lo[s, to, :] = low
            return carry

        lax.fori_loop(0, LIVE, one, 0)

    def multiply(e, dc, p):
        s = owner[e, dc]
        t = t_all[s, part(p), :]
        high = t.astype(jnp.bfloat16)
        low = (t - high.astype(jnp.float32)).astype(jnp.bfloat16)
        both = jnp.dot(jnp.concatenate([high, low], axis=0), v_hi[s], preferred_element_type=jnp.float32)
        more = jnp.dot(high, v_lo[s], preferred_element_type=jnp.float32)
        n = t.shape[0]
        acc[part(p), :] += both[:n] + (both[n:] + more)

    def pass_on(e, p):
        arrive(e, 0, p)
        send(owner[e, 0], p, ways(e, p, "ud") + "s")

    def sibling(e, p):
        arrive(e, 1, p)
        multiply(e, 1, p)

    acc[...] = jnp.zeros_like(acc)
    list_copy.wait()
    prepare((0, 0), 0)
    prepare((0, 0), 1)
    for p in range(PIECES):
        multiply((0, 0), 0, p)
    for p in range(PIECES):
        sibling((0, 0), p)
    for e in FIRST:
        prepare(e, 0)
        prepare(e, 1)
    hear(0)
    tell(1)
    for p in range(PIECES):
        for e in FIRST:
            arrive(e, 0, p)
            send(owner[e, 0], p, ways(e, p, "x"))
            send(owner[e, 0], p, ways(e, p, "ud"))
        send(owner[(1, 0), 0], p, ways((1, 0), p, "2"))
        for e in FIRST:
            send(owner[e, 0], p, "s")
    for e in LATE:
        prepare(e, 0)
        prepare(e, 1)
    hear(1)
    tell(2)
    for e in FIRST:
        multiply(e, 0, 0)
    for e in FIRST:
        sibling(e, 0)
    hear(2)

    def over_y(k, at, q):
        return pltpu.make_async_remote_copy(
            src_ref=acc.at[part(0)], dst_ref=sum_y.at[at], send_sem=y_out.at[k], recv_sem=y_got.at[at],
            device_id={"row": q}, device_id_type=MESH)

    def over_x(at):
        return pltpu.make_async_remote_copy(
            src_ref=sum_x.at[at], dst_ref=sum_x.at[at], send_sem=x_out.at[0], recv_sem=x_got.at[at],
            device_id={"row": row_of(0, 1)}, device_id_type=MESH)

    def over_all(k, at, q):
        return pltpu.make_async_remote_copy(
            src_ref=acc.at[part(1)], dst_ref=sum_all.at[at], send_sem=all_out.at[k], recv_sem=all_got.at[at],
            device_id={"row": q}, device_id_type=MESH)

    sums = [over_y(k, y, row_of(k, 0)) for k in range(1, 4)]
    for e in LATE:
        pass_on(e, 0)
    for e in LATE:
        multiply(e, 0, 0)
    for e in LATE:
        sibling(e, 0)
    for copy in sums:
        copy.start()
    sum_y[y] = acc[part(0), :]
    for e in LATE:
        pass_on(e, 1)
    for e in FIRST:
        multiply(e, 0, 1)
    for e in FIRST:
        sibling(e, 1)
    for e in LATE:
        multiply(e, 0, 1)
    for e in LATE:
        sibling(e, 1)
    far = ((2, 1), (1, 1), (3, 1), (2, 0), (0, 1), (1, 0), (3, 0))
    last = [over_all(k, row, row_of(*far[k - 1])) for k in range(1, rows)]
    for copy in last:
        copy.start()
    sum_all[row] = acc[part(1), :]
    for k in range(1, 4):
        over_y(k, lax.rem(y + k, 4), row_of(k, 0)).wait_recv()
    sum_x[x_hi] = (sum_y[0] + sum_y[1]) + (sum_y[2] + sum_y[3])
    across = over_x(x_hi)
    across.start()
    for copy in sent + sums + last:
        copy.wait_send()
    for k in range(1, rows):
        q = lax.rem(row + k, rows)
        over_all(k, q, q).wait_recv()
    total = sum_all[0]
    for q in range(1, rows):
        total = total + sum_all[q]
    o_ref[part(1), :] = total
    over_x(1 - x_hi).wait_recv()
    o_ref[part(0), :] = sum_x[0] + sum_x[1]
    across.wait_send()


def per_device(rows, amplitudes, ladder_ints, tile_mask):
    return pl.pallas_call(
        functools.partial(kernel, rows),
        out_shape=jax.ShapeDtypeStruct((64, 256), jnp.float32),
        in_specs=[pl.BlockSpec(memory_space=pl.ANY)] * 3,
        out_specs=pl.BlockSpec(memory_space=pltpu.VMEM),
        scratch_shapes=[
            pltpu.VMEM((64, 1024), jnp.float32),
            pltpu.VMEM((64, 256), jnp.int32),
            pltpu.VMEM((8, 256), jnp.int32),
            pltpu.SMEM((8, 256), jnp.int32),
            pltpu.VMEM((16, LIVE * TILE, 256), jnp.bfloat16),
            pltpu.VMEM((16, LIVE * TILE, 256), jnp.bfloat16),
            pltpu.VMEM((16, 64, 512), jnp.float32),
            pltpu.VMEM((64, 256), jnp.float32),
            pltpu.VMEM((4, ROWS[1], 256), jnp.float32),
            pltpu.VMEM((2, ROWS[1], 256), jnp.float32),
            pltpu.VMEM((rows, 64 - ROWS[1], 256), jnp.float32),
            pltpu.SemaphoreType.DMA((3,)),
            pltpu.SemaphoreType.DMA((16,)),
            pltpu.SemaphoreType.DMA((N_SENT,)),
            pltpu.SemaphoreType.DMA((16 * PIECES,)),
            pltpu.SemaphoreType.DMA((4,)),
            pltpu.SemaphoreType.DMA((4,)),
            pltpu.SemaphoreType.DMA((1,)),
            pltpu.SemaphoreType.DMA((2,)),
            pltpu.SemaphoreType.DMA((rows,)),
            pltpu.SemaphoreType.DMA((rows,)),
            pltpu.SemaphoreType.REGULAR((ROUNDS,)),
        ] + [pltpu.VMEM((1024, 256), jnp.float32)] * 16,
        compiler_params=pltpu.CompilerParams(
            collective_id=0, has_side_effects=True, vmem_limit_bytes=60 * 1024 * 1024),
    )(amplitudes, ladder_ints, tile_mask.T)


def solution(mesh):
    in_specs = (P(None, ("row", "col")), P("row", "col"), P())
    out_specs = P(None, "col")
    return jax.shard_map(
        functools.partial(per_device, mesh.shape["row"]), mesh=mesh, in_specs=in_specs, out_specs=out_specs,
        check_vma=False)
```

```python
import functools

import jax
import jax.numpy as jnp
from jax import lax
from jax.experimental import pallas as pl
from jax.experimental.pallas import tpu as pltpu
from jax.sharding import PartitionSpec as P

TILE = 64
GROUP = 16
LIVE = 8
PIECES = 2
ROWS = (0, 32, 64)
MESH = pl.DeviceIdType.MESH

TREES = ({(0, 0): "udx", (0, 1): "xu", (0, 3): "x", (1, 0): "2"}, {(0, 0): "udx", (0, 3): "xd", (1, 0): "u2"})
FIRST = ((0, 1), (0, 3), (1, 0))
SECOND = ((1, 1), (1, 3), (1, 2))
LATE = ((0, 2), (1, 1), (1, 3), (1, 2))
ORDER = ((0, 0),) + FIRST + LATE
N_SENT = 15 * PIECES
ROUNDS = 3


def kernel(rows, t_hbm, v_hbm, m_hbm, o_ref, t_in, m_in, list_v, list_s, v_hi, v_lo, t_all, acc, sum_y, sum_x, sum_all,
           in_sem, v_sem, out_sem, got_sem, y_out, y_got, x_out, x_got, all_out, all_got, near_sem, *v_in):
    row = lax.axis_index("row")
    col = lax.axis_index("col")
    core = lax.rem(col, 2)
    z = lax.rem(lax.div(col, 2), 4)
    x_lo = lax.div(col, 8)
    y = lax.div(row, 2)
    x_hi = lax.rem(row, 2)

    def col_of(dx, dz, dc):
        return lax.rem(x_lo + dx, 2) * 8 + lax.rem(z + dz, 4) * 2 + lax.rem(core + dc, 2)

    def row_of(dy, dx):
        return lax.rem(y + dy, 4) * 2 + lax.rem(x_hi + dx, 2)

    link = {"u": col_of(0, 1, 0), "d": col_of(0, 3, 0), "2": col_of(0, 2, 0), "x": col_of(1, 0, 0),
            "s": col_of(0, 0, 1)}
    near = ({"row": row_of(1, 0)}, {"row": row_of(3, 0)}, {"col": link["x"]}, {"row": row_of(0, 1), "col": link["x"]})

    mask_copy = pltpu.make_async_copy(
        m_hbm.at[:, pl.ds(pl.multiple_of(row * 256, 256), 256)], m_in, in_sem.at[0])
    mask_copy.start()
    t_copy = pltpu.make_async_copy(t_hbm, t_in, in_sem.at[1])
    t_copy.start()

    barrier = pltpu.get_barrier_semaphore()
    for to in [{"col": link[way]} for way in "ud2s"] + list(near):
        pl.semaphore_signal(barrier, inc=1, device_id=to, device_id_type=MESH)

    owner = {(e, dc): col_of(e[0], (4 - e[1]) % 4, dc) for e in ORDER for dc in (0, 1)}
    v_of = dict(zip(owner, v_in))
    v_copies = {}
    for n, at in enumerate(owner):
        v_copies[at] = pltpu.make_async_copy(
            v_hbm.at[pl.ds(pl.multiple_of(owner[at] * 1024, 1024), 1024), :], v_of[at], v_sem.at[n])
        v_copies[at].start()

    mask_copy.wait()
    live = jnp.broadcast_to(jnp.max(m_in[...], axis=0, keepdims=True), (8, 256))
    lane = lax.broadcasted_iota(jnp.int32, (8, 256), 1)
    slot = lax.broadcasted_iota(jnp.int32, (8, 256), 0)
    tile = lane & 15
    count = live
    for s in (1, 2, 4, 8):
        count = count + jnp.where(tile >= s, pltpu.roll(count, s, 1), 0)
    place = jnp.where(live > 0, count - 1, 15 - tile + count)
    mine = m_in[pl.ds(pl.multiple_of(lax.div(col, 2) * 8, 8), 8), :]
    bit = slot - lax.rem(col, 2) * 4
    weight = jnp.where(bit == 0, 16, jnp.where(bit == 1, 32, jnp.where(bit == 2, 64, jnp.where(bit == 3, 128, 0))))
    code = jnp.sum(mine * weight, axis=0, keepdims=True)
    entry = jnp.where(place == slot, tile + code, 0)
    for s in (1, 2, 4, 8):
        entry = entry + pltpu.roll(entry, 256 - s, 1)
    list_v[...] = entry
    list_copy = pltpu.make_async_copy(list_v, list_s, in_sem.at[2])
    list_copy.start()
    own = jnp.broadcast_to(pltpu.roll(entry, lax.rem(256 - col * GROUP, 256), 1)[:, :1], (8, 128)) & 15
    t_copy.wait()

    sent = []

    def part(p):
        return pl.ds(ROWS[p], ROWS[p + 1] - ROWS[p])

    left = lax.broadcasted_iota(jnp.int32, (1, 128), 1) < TILE

    def pack(p):
        for n in range(LIVE // 2):
            halves = []
            for h in (0, 1):
                at = own[2 * n + h:2 * n + h + 1]
                block = t_in[part(p), 7 * 128:]
                for b in range(n, 7):
                    block = jnp.where(at >> 1 == b, t_in[part(p), b * 128:(b + 1) * 128], block)
                halves.append(jnp.where(at & 1 != h, pltpu.roll(block, TILE, 1), block))
            t_all[col, part(p), n * 128:n * 128 + 128] = jnp.where(left, halves[0], halves[1])

    def piece(s, p, to, n):
        return pltpu.make_async_remote_copy(
            src_ref=t_all.at[s, part(p)], dst_ref=t_all.at[s, part(p)], send_sem=out_sem.at[n],
            recv_sem=got_sem.at[s * PIECES + p], device_id={"col": to}, device_id_type=MESH)

    def send(s, p, ways):
        for way in ways:
            copy = piece(s, p, link[way], len(sent))
            copy.start()
            sent.append(copy)

    def arrive(e, dc, p):
        piece(owner[e, dc], p, link["s"], 0).wait_recv()

    def ways(e, p, which):
        return "".join(w for w in TREES[p % len(TREES)].get(e, "") if w in which)

    pack(0)
    pl.semaphore_wait(barrier, 8)
    send(col, 0, "udx")
    pack(1)
    send(col, 1, "udx")
    for p in range(PIECES):
        send(col, p, "s")

    def tell(n):
        for to in near:
            pl.semaphore_signal(near_sem.at[n], inc=1, device_id=to, device_id_type=MESH)

    def hear(n):
        pl.semaphore_wait(near_sem.at[n], len(near))

    tell(0)

    bits = 16 << lax.div(lax.broadcasted_iota(jnp.int32, (1, 256), 1), TILE)

    def prepare(e, dc):
        s = owner[e, dc]
        v_copies[e, dc].wait()

        def one(k, carry):
            at = list_s[k, s * GROUP]
            tile_rows = v_of[e, dc][pl.ds((at & 15) * TILE, TILE), :]
            tile_rows = jnp.where((jnp.full((1, 256), at, jnp.int32) & bits) != 0, tile_rows, 0.0)
            high = tile_rows.astype(jnp.bfloat16)
            low = (tile_rows - high.astype(jnp.float32)).astype(jnp.bfloat16)
            to = pl.ds(pl.multiple_of(k * TILE, TILE), TILE)
            v_hi[s, to, :] = high
            v_lo[s, to, :] = low
            return carry

        lax.fori_loop(0, LIVE, one, 0)

    def multiply(e, dc, p):
        s = owner[e, dc]
        t = t_all[s, part(p), :]
        high = t.astype(jnp.bfloat16)
        low = (t - high.astype(jnp.float32)).astype(jnp.bfloat16)
        both = jnp.dot(jnp.concatenate([high, low], axis=0), v_hi[s], preferred_element_type=jnp.float32)
        more = jnp.dot(high, v_lo[s], preferred_element_type=jnp.float32)
        n = t.shape[0]
        acc[part(p), :] += both[:n] + (both[n:] + more)

    def pass_on(e, p):
        arrive(e, 0, p)
        send(owner[e, 0], p, ways(e, p, "ud") + "s")

    def sibling(e, p):
        arrive(e, 1, p)
        multiply(e, 1, p)

    acc[...] = jnp.zeros_like(acc)
    list_copy.wait()
    prepare((0, 0), 0)
    prepare((0, 0), 1)
    for p in range(PIECES):
        multiply((0, 0), 0, p)
    for p in range(PIECES):
        sibling((0, 0), p)
    for e in FIRST:
        prepare(e, 0)
        prepare(e, 1)
    hear(0)
    tell(1)
    for p in range(PIECES):
        for e in FIRST:
            arrive(e, 0, p)
            send(owner[e, 0], p, ways(e, p, "x"))
            send(owner[e, 0], p, ways(e, p, "ud"))
        send(owner[(1, 0), 0], p, ways((1, 0), p, "2"))
        for e in FIRST:
            send(owner[e, 0], p, "s")
    for e in LATE:
        prepare(e, 0)
        prepare(e, 1)
    hear(1)
    tell(2)
    for e in FIRST:
        multiply(e, 0, 0)
    for e in FIRST:
        sibling(e, 0)
    hear(2)

    def over_y(k, at, q):
        return pltpu.make_async_remote_copy(
            src_ref=acc.at[part(0)], dst_ref=sum_y.at[at], send_sem=y_out.at[k], recv_sem=y_got.at[at],
            device_id={"row": q}, device_id_type=MESH)

    def over_x(at):
        return pltpu.make_async_remote_copy(
            src_ref=sum_x.at[at], dst_ref=sum_x.at[at], send_sem=x_out.at[0], recv_sem=x_got.at[at],
            device_id={"row": row_of(0, 1)}, device_id_type=MESH)

    def over_all(k, at, q):
        return pltpu.make_async_remote_copy(
            src_ref=acc.at[part(1)], dst_ref=sum_all.at[at], send_sem=all_out.at[k], recv_sem=all_got.at[at],
            device_id={"row": q}, device_id_type=MESH)

    sums = [over_y(k, y, row_of(k, 0)) for k in range(1, 4)]
    for e in LATE:
        pass_on(e, 0)
    for e in LATE:
        multiply(e, 0, 0)
    for e in LATE:
        sibling(e, 0)
    for copy in sums:
        copy.start()
    sum_y[y] = acc[part(0), :]
    for e in LATE:
        pass_on(e, 1)
    for e in FIRST:
        multiply(e, 0, 1)
    for e in FIRST:
        sibling(e, 1)
    for e in LATE:
        multiply(e, 0, 1)
    for e in LATE:
        sibling(e, 1)
    far = ((2, 1), (1, 1), (3, 1), (2, 0), (0, 1), (1, 0), (3, 0))
    last = [over_all(k, row, row_of(*far[k - 1])) for k in range(1, rows)]
    for copy in last:
        copy.start()
    sum_all[row] = acc[part(1), :]
    for k in range(1, 4):
        over_y(k, lax.rem(y + k, 4), row_of(k, 0)).wait_recv()
    sum_x[x_hi] = (sum_y[0] + sum_y[1]) + (sum_y[2] + sum_y[3])
    across = over_x(x_hi)
    across.start()
    for copy in sent + sums + last:
        copy.wait_send()
    total = None
    for q in range(rows):
        @pl.when(row != q)
        def _():
            over_all(1, q, q).wait_recv()
        total = sum_all[q] if total is None else total + sum_all[q]
    o_ref[part(1), :] = total
    over_x(1 - x_hi).wait_recv()
    o_ref[part(0), :] = sum_x[0] + sum_x[1]
    across.wait_send()


def per_device(rows, amplitudes, ladder_ints, tile_mask):
    return pl.pallas_call(
        functools.partial(kernel, rows),
        out_shape=jax.ShapeDtypeStruct((64, 256), jnp.float32),
        in_specs=[pl.BlockSpec(memory_space=pl.ANY)] * 3,
        out_specs=pl.BlockSpec(memory_space=pltpu.VMEM),
        scratch_shapes=[
            pltpu.VMEM((64, 1024), jnp.float32),
            pltpu.VMEM((64, 256), jnp.int32),
            pltpu.VMEM((8, 256), jnp.int32),
            pltpu.SMEM((8, 256), jnp.int32),
            pltpu.VMEM((16, LIVE * TILE, 256), jnp.bfloat16),
            pltpu.VMEM((16, LIVE * TILE, 256), jnp.bfloat16),
            pltpu.VMEM((16, 64, 512), jnp.float32),
            pltpu.VMEM((64, 256), jnp.float32),
            pltpu.VMEM((4, ROWS[1], 256), jnp.float32),
            pltpu.VMEM((2, ROWS[1], 256), jnp.float32),
            pltpu.VMEM((rows, 64 - ROWS[1], 256), jnp.float32),
            pltpu.SemaphoreType.DMA((3,)),
            pltpu.SemaphoreType.DMA((16,)),
            pltpu.SemaphoreType.DMA((N_SENT,)),
            pltpu.SemaphoreType.DMA((16 * PIECES,)),
            pltpu.SemaphoreType.DMA((4,)),
            pltpu.SemaphoreType.DMA((4,)),
            pltpu.SemaphoreType.DMA((1,)),
            pltpu.SemaphoreType.DMA((2,)),
            pltpu.SemaphoreType.DMA((rows,)),
            pltpu.SemaphoreType.DMA((rows,)),
            pltpu.SemaphoreType.REGULAR((ROUNDS,)),
        ] + [pltpu.VMEM((1024, 256), jnp.float32)] * 16,
        compiler_params=pltpu.CompilerParams(
            collective_id=0, has_side_effects=True, vmem_limit_bytes=60 * 1024 * 1024),
    )(amplitudes, ladder_ints, tile_mask.T)


def solution(mesh):
    in_specs = (P(None, ("row", "col")), P("row", "col"), P())
    out_specs = P(None, "col")
    return jax.shard_map(
        functools.partial(per_device, mesh.shape["row"]), mesh=mesh, in_specs=in_specs, out_specs=out_specs,
        check_vma=False)
```
